512 devices in a mesh: seq: 64 (over z, y), rep: 8 (over x, core).
Axes of the slice: x: 4, y: 4, z: 16, core: 2. Of those that a mesh axis runs over, the one named last changes fastest.
Arguments:
- queries: bfloat16 [8, 8192, 1024], P('rep', 'seq'), may hold values from -6.5 to 6.5
- keys: bfloat16 [8, 8192, 128], P('rep', 'seq'), may hold values from -4 to 4
- values: bfloat16 [8, 8192, 128], P('rep', 'seq'), may hold values from -5 to 5
- out_grad: bfloat16 [8, 8192, 1024], P('rep', 'seq'), may hold values from -5 to 5
- q_bias: float32 [1024], replicated, may hold values from -3 to 3
- v_bias: float32 [128], replicated, may hold values from -3 to 3
- doc_lengths: int32 [8, 16], P('rep'), may hold values from 1 to 897, 8192 in all within a row
Outputs:
- attended: bfloat16 [8, 8192, 1024], P('rep', 'seq')
- q_grad: float32 [8, 8192, 1024], P('rep', 'seq')
- k_grad: float32 [8, 8192, 128], P('rep', 'seq')
- v_grad: float32 [8, 8192, 128], P('rep', 'seq')
- q_bias_grad: float32 [1024], replicated
- v_bias_grad: float32 [128], replicated
The draws below stay inside these ranges and needn't reach their ends.
Inputs may be any that keep to these rules, and one draw needn't show every extreme that they name: `doc_lengths`: each micro-batch holds 16 documents in order whose lengths sum to 8192; the longest is exactly 897 tokens.
All inputs are finite; a program needn't handle non-finite values.
Results may differ from the reference program's by a relative error of at most 0.04.
Values may be sent and summed in bfloat16 or wider, within the bound.
No kernel may reach another device: no remote copies, remote signals or barrier semaphores. Data moves between devices by JAX's collectives and lax.ppermute only.
A program may use at most 64 MiB of HBM per device.

```python
import math
import jax
import jax.numpy as jnp
import numpy as np
from jax import lax

HEADS = 8
HEAD_DIM = 128
TOK_DEV = 128
SPAN = 8
BATCH = 8
S = 8192
DOCS = 16
MOST = 897


def shared_keys(key):
    base_draw = jnp.clip(jax.random.normal(jax.random.fold_in(key, 101), (BATCH, S, HEAD_DIM), jnp.float32), -4.0, 4.0)
    return base_draw


def draw_keys(key, part):
    base_draw = shared_keys(key)
    return base_draw.astype(jnp.bfloat16)


def draw_queries(key, part):
    key = jax.random.fold_in(key, 5)
    base_draw = jnp.clip(jax.random.normal(key, (BATCH, S, HEADS * HEAD_DIM), jnp.float32), -4.0, 4.0)
    return base_draw.astype(jnp.bfloat16)


def block_levels(own_key, dims, shards, smallest, top_value):
    factor_of = 1.0
    for position, blocks in shards:
        heights = jax.random.uniform(jax.random.fold_in(jax.random.fold_in(own_key, 6), position), (blocks,), jnp.float32, smallest / len(shards), top_value / len(shards))
        factor_of = factor_of * jnp.repeat(jnp.exp(heights), dims[position] // blocks).reshape((-1,) + (1,) * (len(dims) - 1 - position))
    return factor_of


def length_profile(number_of, total, most, lean):
    weights = [(1 << 20) // math.isqrt(standing ** lean) + 1 for standing in range(2, number_of + 1)]
    spare, counts = total - most - (number_of - 1), [1] * (number_of - 1)
    while spare > 0:
        candidates = [i for i in range(number_of - 1) if counts[i] < most]
        whole, budget = sum([weights[i] for i in candidates]), spare
        for i in candidates:
            extra = min(most - counts[i], max(1, budget * weights[i] // whole), spare)
            counts[i] = counts[i] + extra
            spare = spare - extra
    return np.array([most] + counts)


def ragged(key, amount, total, bound, skew):
    if amount == 2:
        one = jax.random.randint(key, (), max(1, total - bound), min(bound, total - 1) + 1)
        return jnp.stack([one, total - one])
    sizes = jnp.asarray(length_profile(amount, total, bound, skew), jnp.int32)
    couples = (amount - 1) // 2
    source_of, taker = sizes[1:1 + 2 * couples:2], sizes[2:2 + 2 * couples:2]
    room = jnp.minimum(source_of - 1, bound - taker)
    moved = jax.random.randint(jax.random.fold_in(key, 1), (couples,), 0, 1 << 20) % (room + 1)
    sizes = sizes.at[1:1 + 2 * couples:2].set(source_of - moved).at[2:2 + 2 * couples:2].set(taker + moved)
    return sizes[jax.random.permutation(jax.random.fold_in(key, 2), amount)]


def noise(key, extent, width, most, split=(), kind=jnp.bfloat16):
    values = width * jax.random.normal(key, extent, jnp.float32)
    if split:
        values = values * block_levels(key, extent, split, -0.22, 0.18)
    return jnp.clip(values, -most, most).astype(kind)


def setup_inputs(seed: int = 0) -> dict:
    key_list = jax.random.split(jax.random.key(seed), 8)
    return {
        "queries": draw_queries(jax.random.fold_in(key_list[7], 71), 0),
        "keys": draw_keys(jax.random.fold_in(key_list[7], 71), 0),
        "values": noise(key_list[2], (BATCH, S, HEAD_DIM), 1.0, 5.0, ((0, 8), (1, 64))),
        "out_grad": noise(key_list[3], (BATCH, S, HEADS * HEAD_DIM), 1.0, 5.0, ((0, 8), (1, 64))),
        "q_bias": noise(key_list[4], (HEADS * HEAD_DIM,), 0.5, 3.0, (), jnp.float32),
        "v_bias": noise(key_list[5], (HEAD_DIM,), 0.5, 3.0, (), jnp.float32),
        "doc_lengths": jax.vmap(lambda own: ragged(own, DOCS, S, MOST, 1))(jax.random.split(key_list[6], BATCH)).reshape((BATCH, DOCS)).astype(jnp.int32),
    }


masked_fill = -1e+30

def doc_index(doc_ends, positions):
    return lax.optimization_barrier(jnp.sum((doc_ends[None, :] <= positions[:, None]).astype(jnp.int32), axis=1))

def allowed_mask(doc_ends, query_pos, key_pos):
    same_doc = doc_index(doc_ends, query_pos)[:, None] == doc_index(doc_ends, key_pos)[None, :]
    return same_doc & (key_pos[None, :] <= query_pos[:, None]) & (key_pos[None, :] >= 0)

def reference(queries, keys, values, out_grad, q_bias, v_bias, doc_lengths):
    f32 = jnp.float32
    bf16 = jnp.bfloat16
    score_scale = 1.0 / math.sqrt(HEAD_DIM)
    reach = SPAN * TOK_DEV
    margin = reach - TOK_DEV
    block_total = S // TOK_DEV
    attended_all, q_all, k_all, v_all = ([], [], [], [])
    for batch_index in range(BATCH):
        query_rows = (queries[batch_index].astype(f32) + q_bias.astype(f32)[None, :]).astype(bf16)
        query_rows = query_rows.reshape(S, HEADS, HEAD_DIM)
        value_rows = (values[batch_index].astype(f32) + v_bias.astype(f32)[None, :]).astype(bf16)
        keys_pad = jnp.concatenate([jnp.zeros((margin, HEAD_DIM), bf16), keys[batch_index]], axis=0)
        values_pad = jnp.concatenate([jnp.zeros((margin, HEAD_DIM), bf16), value_rows], axis=0)
        grad_rows = out_grad[batch_index].reshape(S, HEADS, HEAD_DIM)
        doc_ends = jnp.cumsum(doc_lengths[batch_index]).astype(jnp.int32)

        def step(carry, block_index):
            key_acc, value_acc = carry
            start = (block_index * TOK_DEV).astype(jnp.int32)
            q_block = lax.dynamic_slice_in_dim(query_rows, start, TOK_DEV, 0)
            d_block = lax.dynamic_slice_in_dim(grad_rows, start, TOK_DEV, 0)
            k_window = lax.dynamic_slice_in_dim(keys_pad, start, reach, 0)
            v_window = lax.dynamic_slice_in_dim(values_pad, start, reach, 0)
            query_pos = start + jnp.arange(TOK_DEV, dtype=jnp.int32)
            key_pos = start - margin + jnp.arange(reach, dtype=jnp.int32)
            allowed = allowed_mask(doc_ends, query_pos, key_pos)[None]
            scores = jnp.einsum('thd,kd->htk', q_block.astype(f32), k_window.astype(f32)) * score_scale
            scores = jnp.where(allowed, scores, masked_fill)
            top = lax.optimization_barrier(jnp.max(scores, axis=2, keepdims=True))
            total = lax.optimization_barrier(jnp.sum(jnp.where(allowed, jnp.exp(scores - top), 0.0), axis=2, keepdims=True))
            log_norm = top + jnp.log(total)
            weights = jnp.where(allowed, jnp.exp(scores - log_norm), 0.0)
            probs = weights.astype(bf16)
            attended = jnp.einsum('htk,kd->thd', probs.astype(f32), v_window.astype(f32)).astype(bf16)
            delta = jnp.einsum('thd,thd->ht', d_block.astype(f32), attended.astype(f32))
            d_probs = jnp.einsum('thd,kd->htk', d_block.astype(f32), v_window.astype(f32))
            d_scores = (weights * (d_probs - delta[:, :, None]) * score_scale).astype(bf16)
            q_grad = jnp.einsum('htk,kd->thd', d_scores.astype(f32), k_window.astype(f32))
            k_term = jnp.einsum('htk,thd->kd', d_scores.astype(f32), q_block.astype(f32))
            v_term = jnp.einsum('htk,thd->kd', probs.astype(f32), d_block.astype(f32))
            key_acc = lax.dynamic_update_slice_in_dim(key_acc, lax.dynamic_slice_in_dim(key_acc, start, reach, 0) + k_term, start, 0)
            value_acc = lax.dynamic_update_slice_in_dim(value_acc, lax.dynamic_slice_in_dim(value_acc, start, reach, 0) + v_term, start, 0)
            return ((key_acc, value_acc), (attended.reshape(TOK_DEV, HEADS * HEAD_DIM), q_grad.reshape(TOK_DEV, HEADS * HEAD_DIM)))
        empty = jnp.zeros((S + margin, HEAD_DIM), f32)
        (key_acc, value_acc), (attended, q_grad) = lax.scan(step, (empty, empty), jnp.arange(block_total, dtype=jnp.int32))
        attended_all.append(attended.reshape(S, HEADS * HEAD_DIM))
        q_all.append(q_grad.reshape(S, HEADS * HEAD_DIM))
        k_all.append(key_acc[margin:])
        v_all.append(value_acc[margin:])
    attended_out = jnp.stack(attended_all)
    q_grad_out = jnp.stack(q_all)
    k_grad_out = jnp.stack(k_all)
    v_grad_out = jnp.stack(v_all)
    inverse = 1.0 / math.sqrt(BATCH * S)
    q_bias_grad = lax.optimization_barrier(jnp.sum(q_grad_out, axis=(0, 1))) * inverse
    v_bias_grad = lax.optimization_barrier(jnp.sum(v_grad_out, axis=(0, 1))) * inverse
    return (attended_out, q_grad_out, k_grad_out, v_grad_out, q_bias_grad, v_bias_grad)
```

```python
import functools
import math

import jax
import jax.numpy as jnp
from jax import lax
from jax.experimental import pallas as pl
from jax.experimental.pallas import tpu as pltpu
from jax.sharding import Mesh
from jax.sharding import PartitionSpec as P

SPAN = 8
HEAD_GROUP = 2
masked_fill = -1e30
f32 = jnp.float32
bf16 = jnp.bfloat16


def transposed_product(a, b):
    return lax.dot_general(a, b, (((1,), (1,)), ((), ())), preferred_element_type=f32)


def attention_kernel(
    place, lengths, queries, out_grad, window, q_bias, v_bias,
    attended, q_grad, partials, q_sum, v_sum,
    value_rows, value_cols, key_cols, fill, key_acc, value_acc,
):
    tokens, head_dim = queries.shape[0], v_bias.shape[1]
    heads = queries.shape[1] // head_dim
    span = window.shape[0]
    reach = span * tokens
    scale = 1.0 / math.sqrt(head_dim)
    shard, member = place[0], place[1]

    query_pos = shard * tokens + lax.broadcasted_iota(jnp.int32, (1, tokens), 1)
    first = jnp.zeros((1, tokens), jnp.int32)
    end = jnp.int32(0)
    for doc in range(lengths.shape[1]):
        end = end + lengths[0, doc]
        first = jnp.where(end <= query_pos, end, first)

    for slot in range(span):
        rows = pl.ds(slot * tokens, tokens)
        owner = shard - member + slot - jnp.where(slot > member, span, 0)
        key_pos = owner * tokens + lax.broadcasted_iota(jnp.int32, (tokens, tokens), 0)
        allowed = (key_pos >= first) & (key_pos <= query_pos)
        fill[rows, :] = jnp.where(allowed, 0.0, masked_fill)
        values = (window[slot, :, head_dim:].astype(f32) + v_bias[...]).astype(bf16)
        value_rows[rows, :] = values
        value_cols[:, rows] = values.T
        key_cols[:, rows] = window[slot, :, :head_dim].T

    keys = window[:, :, :head_dim].reshape(reach, head_dim)
    fill_pair = jnp.concatenate([fill[...]] * HEAD_GROUP, axis=1)
    for first_head in range(0, heads, HEAD_GROUP):
        cols = [pl.ds((first_head + n) * head_dim, head_dim) for n in range(HEAD_GROUP)]
        query_rows = jnp.concatenate(
            [(queries[:, c].astype(f32) + q_bias[:, c]).astype(bf16) for c in cols], axis=0
        )
        grad_rows = jnp.concatenate([out_grad[:, c] for c in cols], axis=0)
        scores = transposed_product(keys, query_rows) * (scale * math.log2(math.e)) + fill_pair
        top = jnp.max(scores, axis=0, keepdims=True)
        powers = jnp.exp2(scores - top)
        weights = powers * (1.0 / jnp.sum(powers, axis=0, keepdims=True))
        probs = weights.astype(bf16)
        found = jnp.dot(value_cols[...], probs, preferred_element_type=f32).astype(bf16)
        grad_cols = grad_rows.T
        delta = jnp.sum(grad_cols.astype(f32) * found.astype(f32), axis=0, keepdims=True)
        d_probs = transposed_product(value_rows[...], grad_rows)
        d_scores = (weights * (d_probs - delta)).astype(bf16)
        q_part = jnp.dot(key_cols[...], d_scores, preferred_element_type=f32).T * scale
        found_rows = found.T
        for n, c in enumerate(cols):
            rows = slice(n * tokens, (n + 1) * tokens)
            attended[:, c] = found_rows[rows]
            q_grad[:, c] = q_part[rows]
            q_sum[:, c] = jnp.sum(q_part[rows], axis=0, keepdims=True)
        key_term = jnp.dot(d_scores, query_rows, preferred_element_type=f32)
        value_term = jnp.dot(probs, grad_rows, preferred_element_type=f32)
        if first_head == 0:
            key_acc[...] = key_term
            value_acc[...] = value_term
        else:
            key_acc[...] += key_term
            value_acc[...] += value_term
    partials[:, :, :head_dim] = (key_acc[...] * scale).astype(bf16).reshape(span, tokens, head_dim)
    partials[:, :, head_dim:] = value_acc[...].astype(bf16).reshape(span, tokens, head_dim)
    v_sum[...] = jnp.sum(value_acc[...], axis=0, keepdims=True)


def attention(place, lengths, queries, out_grad, window, q_bias, v_bias):
    tokens, width = queries.shape
    span, _, pair = window.shape
    head_dim = pair // 2
    reach = span * tokens
    vmem = pl.BlockSpec(memory_space=pltpu.VMEM)
    smem = pl.BlockSpec(memory_space=pltpu.SMEM)
    return pl.pallas_call(
        attention_kernel,
        out_shape=(
            jax.ShapeDtypeStruct((tokens, width), bf16),
            jax.ShapeDtypeStruct((tokens, width), f32),
            jax.ShapeDtypeStruct((span, tokens, pair), bf16),
            jax.ShapeDtypeStruct((1, width), f32),
            jax.ShapeDtypeStruct((1, head_dim), f32),
        ),
        in_specs=[smem, smem] + [vmem] * 5,
        out_specs=(vmem,) * 5,
        scratch_shapes=[
            pltpu.VMEM((reach, head_dim), bf16),
            pltpu.VMEM((head_dim, reach), bf16),
            pltpu.VMEM((head_dim, reach), bf16),
            pltpu.VMEM((reach, tokens), f32),
            pltpu.VMEM((reach, head_dim), f32),
            pltpu.VMEM((reach, head_dim), f32),
        ],
        compiler_params=pltpu.CompilerParams(vmem_limit_bytes=40 * 1024 * 1024),
        cost_estimate=pl.CostEstimate(
            flops=12 * width * reach * tokens,
            bytes_accessed=4 * tokens * width * 2,
            transcendentals=reach * width,
        ),
        name="attention",
    )(place, lengths, queries, out_grad, window, q_bias, v_bias)


def exchanged(blocks, axis):
    return lax.all_to_all(blocks, axis, 0, 0)


def summed_over(row, axis):
    size = lax.axis_size(axis)
    copies = jnp.broadcast_to(row[None], (size,) + row.shape)
    return jnp.sum(exchanged(copies, axis), axis=0)


def per_device(queries, keys, values, out_grad, q_bias, v_bias, doc_lengths):
    tokens, head_dim = keys.shape[1], keys.shape[2]
    width = queries.shape[2]
    groups, span = lax.axis_size("group"), lax.axis_size("member")
    group, member = lax.axis_index("group"), lax.axis_index("member")
    place = jnp.stack([group * span + member, member]).astype(jnp.int32)

    own = jnp.concatenate([keys[0], values[0]], axis=1)
    before = lax.ppermute(own, "group", [(i, i + 1) for i in range(groups - 1)])
    later = (jnp.arange(span) >= member)[:, None, None]
    window = exchanged(jnp.where(later, own[None], before[None]), "member")

    attended, q_grad, partials, q_sum, v_sum = attention(
        place, doc_lengths, queries[0], out_grad[0], window, q_bias[None], v_bias[None]
    )

    received = exchanged(partials, "member").astype(f32)
    mine = jnp.sum(jnp.where(later, received, 0.0), axis=0)
    others = jnp.sum(jnp.where(later, 0.0, received), axis=0)
    returned = lax.ppermute(others.astype(bf16), "group", [(i + 1, i) for i in range(groups - 1)])
    owned = mine + returned.astype(f32)

    sums = jnp.concatenate([q_sum[0], v_sum[0]])
    for axis in ("rep", "member", "group"):
        sums = summed_over(sums, axis)
    inverse = 1.0 / math.sqrt(groups * span * tokens * lax.axis_size("rep"))
    sums = sums * inverse
    return (
        attended[None],
        q_grad[None],
        owned[None, :, :head_dim],
        owned[None, :, head_dim:],
        sums[:width],
        sums[width:],
    )


def solution(mesh):
    fine = Mesh(
        mesh.devices.reshape(mesh.shape["seq"] // SPAN, SPAN, mesh.shape["rep"]),
        ("group", "member", "rep"),
    )
    tokens = P("rep", ("group", "member"), None)
    return jax.shard_map(
        per_device,
        mesh=fine,
        in_specs=(tokens, tokens, tokens, tokens, P(), P(), P("rep", None)),
        out_specs=(tokens, tokens, tokens, tokens, P(), P()),
        check_vma=False,
    )
```

```python
import functools
import math

import jax
import jax.numpy as jnp
from jax import lax
from jax.experimental import pallas as pl
from jax.experimental.pallas import tpu as pltpu
from jax.sharding import Mesh
from jax.sharding import PartitionSpec as P

SPAN = 8
HEAD_GROUP = 2
SUM_ROWS = 16
masked_fill = -1e30
f32 = jnp.float32
bf16 = jnp.bfloat16


def transposed_product(a, b):
    return lax.dot_general(a, b, (((1,), (1,)), ((), ())), preferred_element_type=f32)


def attention_kernel(
    place, lengths, queries, out_grad, window, q_bias, v_bias,
    attended, q_grad, partials,
    value_rows, value_cols, key_cols, fill, key_acc, value_acc, sum_rows,
):
    step, last = pl.program_id(0), pl.num_programs(0) - 1
    span, _, pair = window.shape
    tokens, head_dim = queries.shape[0], pair // 2
    reach = span * tokens
    scale = 1.0 / math.sqrt(head_dim)
    shard, member = place[0], place[1]

    @pl.when(step == 0)
    def prepare():
        query_pos = shard * tokens + lax.broadcasted_iota(jnp.int32, (1, tokens), 1)
        first = jnp.zeros((1, tokens), jnp.int32)
        end = jnp.int32(0)
        for doc in range(lengths.shape[1]):
            end = end + lengths[0, doc]
            first = jnp.where(end <= query_pos, end, first)

        for slot in range(span):
            rows = pl.ds(slot * tokens, tokens)
            owner = shard - member + slot - jnp.where(slot > member, span, 0)
            key_pos = owner * tokens + lax.broadcasted_iota(jnp.int32, (tokens, tokens), 0)
            allowed = (key_pos >= first) & (key_pos <= query_pos)
            fill[rows, :] = jnp.where(allowed, 0.0, masked_fill)
            values = (window[slot, :, head_dim:].astype(f32) + v_bias[...]).astype(bf16)
            value_rows[rows, :] = values
            value_cols[:, rows] = values.T
            key_cols[:, rows] = window[slot, :, :head_dim].T
        key_acc[...] = jnp.zeros_like(key_acc)
        value_acc[...] = jnp.zeros_like(value_acc)
        sum_rows[...] = jnp.zeros_like(sum_rows)

    keys = window[:, :, :head_dim].reshape(reach, head_dim)
    halves = [slice(n * head_dim, (n + 1) * head_dim) for n in range(HEAD_GROUP)]
    query_rows = jnp.concatenate(
        [(queries[:, c].astype(f32) + q_bias[:, c]).astype(bf16) for c in halves], axis=0
    )
    grad_rows = jnp.concatenate([out_grad[:, c] for c in halves], axis=0)
    fill_pair = jnp.concatenate([fill[...]] * HEAD_GROUP, axis=1)
    scores = transposed_product(keys, query_rows) * (scale * math.log2(math.e)) + fill_pair
    top = jnp.max(scores, axis=0, keepdims=True)
    powers = jnp.exp2(scores - top)
    weights = powers * (1.0 / jnp.sum(powers, axis=0, keepdims=True))
    probs = weights.astype(bf16)
    found = jnp.dot(value_cols[...], probs, preferred_element_type=f32).astype(bf16)
    grad_cols = grad_rows.T
    delta = jnp.sum(grad_cols.astype(f32) * found.astype(f32), axis=0, keepdims=True)
    d_probs = transposed_product(value_rows[...], grad_rows)
    d_scores = (weights * (d_probs - delta)).astype(bf16)
    q_part = jnp.dot(key_cols[...], d_scores, preferred_element_type=f32).T * scale
    found_rows = found.T
    sums = []
    for n, c in enumerate(halves):
        rows = slice(n * tokens, (n + 1) * tokens)
        attended[:, c] = found_rows[rows]
        q_grad[:, c] = q_part[rows]
        sums.append(jnp.sum(q_part[rows], axis=0, keepdims=True))
    key_acc[...] += jnp.dot(d_scores, query_rows, preferred_element_type=f32)
    value_acc[...] += jnp.dot(probs, grad_rows, preferred_element_type=f32)

    def spread(row, value):
        high = value.astype(bf16)
        low = (value - high.astype(f32)).astype(bf16)
        sum_rows[pl.ds(row, 1), :] = high.astype(f32)
        sum_rows[pl.ds(row + SUM_ROWS // 2, 1), :] = low.astype(f32)

    spread(step, jnp.concatenate(sums, axis=1))

    @pl.when(step == last)
    def finish():
        value_sum = jnp.sum(value_acc[...], axis=0, keepdims=True)
        spread(last + 1, jnp.concatenate([value_sum, jnp.zeros_like(value_sum)], axis=1))
        parts = jnp.concatenate([key_acc[...] * scale, value_acc[...]], axis=1).astype(bf16)
        partials[:, :tokens, :] = parts.reshape(span, tokens, pair)
        partials[:, tokens:, :] = jnp.broadcast_to(
            sum_rows[...].astype(bf16)[None], (span, SUM_ROWS, pair)
        )


def attention(place, lengths, queries, out_grad, window, q_bias, v_bias):
    tokens, width = queries.shape
    span, _, pair = window.shape
    head_dim = pair // 2
    reach = span * tokens
    step_cols = HEAD_GROUP * head_dim
    smem = pl.BlockSpec(memory_space=pltpu.SMEM)
    head_cols = pl.BlockSpec((tokens, step_cols), lambda i: (0, i))

    def whole(*shape):
        return pl.BlockSpec(shape, lambda i: (0,) * len(shape))

    return pl.pallas_call(
        attention_kernel,
        grid=(width // step_cols,),
        out_shape=(
            jax.ShapeDtypeStruct((tokens, width), bf16),
            jax.ShapeDtypeStruct((tokens, width), f32),
            jax.ShapeDtypeStruct((span, tokens + SUM_ROWS, pair), bf16),
        ),
        in_specs=[
            smem,
            smem,
            head_cols,
            head_cols,
            whole(span, tokens, pair),
            pl.BlockSpec((1, step_cols), lambda i: (0, i)),
            whole(1, head_dim),
        ],
        out_specs=(head_cols, head_cols, whole(span, tokens + SUM_ROWS, pair)),
        scratch_shapes=[
            pltpu.VMEM((reach, head_dim), bf16),
            pltpu.VMEM((head_dim, reach), bf16),
            pltpu.VMEM((head_dim, reach), bf16),
            pltpu.VMEM((reach, tokens), f32),
            pltpu.VMEM((reach, head_dim), f32),
            pltpu.VMEM((reach, head_dim), f32),
            pltpu.VMEM((SUM_ROWS, pair), f32),
        ],
        compiler_params=pltpu.CompilerParams(vmem_limit_bytes=40 * 1024 * 1024),
        cost_estimate=pl.CostEstimate(
            flops=12 * width * reach * tokens,
            bytes_accessed=4 * tokens * width * 2,
            transcendentals=reach * width,
        ),
        name="attention",
    )(place, lengths, queries, out_grad, window, q_bias, v_bias)


def combine_kernel(place, received, mine, others, sums):
    span, rows, _ = received.shape
    tokens = rows - SUM_ROWS
    member = place[1]
    own = jnp.zeros(mine.shape, f32)
    other = jnp.zeros(mine.shape, f32)
    sum_rows = jnp.zeros((SUM_ROWS, received.shape[2]), f32)
    for slot in range(span):
        part = received[slot, :tokens, :].astype(f32)
        own += jnp.where(slot >= member, part, 0.0)
        other += jnp.where(slot >= member, 0.0, part)
        sum_rows += received[slot, tokens:, :].astype(f32)
    mine[...] = own
    others[...] = other.astype(bf16)
    whole_rows = sum_rows[: SUM_ROWS // 2] + sum_rows[SUM_ROWS // 2 :]
    pair = received.shape[2]
    for copy in range(sums.shape[0]):
        for start in range(0, sums.shape[2], pair):
            size = min(pair, sums.shape[2] - start)
            row = start // pair
            sums[copy, :, start : start + size] = whole_rows[row : row + 1, :size]


def combine(place, received, copies, width):
    span, rows, pair = received.shape
    vmem = pl.BlockSpec(memory_space=pltpu.VMEM)
    return pl.pallas_call(
        combine_kernel,
        out_shape=(
            jax.ShapeDtypeStruct((rows - SUM_ROWS, pair), f32),
            jax.ShapeDtypeStruct((rows - SUM_ROWS, pair), bf16),
            jax.ShapeDtypeStruct((copies, 1, width), f32),
        ),
        in_specs=[pl.BlockSpec(memory_space=pltpu.SMEM), vmem],
        out_specs=(vmem,) * 3,
        name="combine",
    )(place, received)


def exchanged(blocks, axis):
    return lax.all_to_all(blocks, axis, 0, 0)


def per_device(queries, keys, values, out_grad, q_bias, v_bias, doc_lengths):
    tokens, head_dim = keys.shape[1], keys.shape[2]
    width = queries.shape[2]
    groups, span = lax.axis_size("group"), lax.axis_size("member")
    group, member = lax.axis_index("group"), lax.axis_index("member")
    place = jnp.stack([group * span + member, member]).astype(jnp.int32)

    own = jnp.concatenate([keys[0], values[0]], axis=1)
    before = lax.ppermute(own, "group", [(i, i + 1) for i in range(groups - 1)])
    later = (jnp.arange(span) >= member)[:, None, None]
    window = exchanged(jnp.where(later, own[None], before[None]), "member")

    attended, q_grad, partials = attention(
        place, doc_lengths, queries[0], out_grad[0], window, q_bias[None], v_bias[None]
    )

    received = exchanged(partials, "member")
    mine, others, copies = combine(place, received, lax.axis_size("rep"), width + head_dim)
    returned = lax.ppermute(others, "group", [(i + 1, i) for i in range(groups - 1)])
    owned = mine + returned.astype(f32)

    rep_sums = jnp.sum(exchanged(copies, "rep"), axis=0)
    rep_sums, owned = lax.optimization_barrier((rep_sums, owned))
    copies = jnp.broadcast_to(rep_sums[None], (groups,) + rep_sums.shape)
    sums = jnp.sum(exchanged(copies, "group"), axis=(0, 1))
    inverse = 1.0 / math.sqrt(groups * span * tokens * lax.axis_size("rep"))
    sums = sums * inverse
    return (
        attended[None],
        q_grad[None],
        owned[None, :, :head_dim],
        owned[None, :, head_dim:],
        sums[:width],
        sums[width:],
    )


def solution(mesh):
    fine = Mesh(
        mesh.devices.reshape(mesh.shape["seq"] // SPAN, SPAN, mesh.shape["rep"]),
        ("group", "member", "rep"),
    )
    tokens = P("rep", ("group", "member"), None)
    return jax.shard_map(
        per_device,
        mesh=fine,
        in_specs=(tokens, tokens, tokens, tokens, P(), P(), P("rep", None)),
        out_specs=(tokens, tokens, tokens, tokens, P(), P()),
        check_vma=False,
    )
```

```python
import functools
import math

import jax
import jax.numpy as jnp
from jax import lax
from jax.experimental import pallas as pl
from jax.experimental.pallas import tpu as pltpu
from jax.sharding import Mesh
from jax.sharding import PartitionSpec as P

SPAN = 8
HEAD_GROUP = 2
SEQ = ("z", "y")
MEMBER_FIRST = 0
LINE_FIRST = 5
SUM_ROWS = 16
masked_fill = -1e30
f32 = jnp.float32
bf16 = jnp.bfloat16


def transposed_product(a, b):
    return lax.dot_general(a, b, (((1,), (1,)), ((), ())), preferred_element_type=f32)


def attention_kernel(
    place, queries, out_grad, window, bias,
    attended, q_grad, partials,
    value_rows, key_cols, value_cols, fill, score, power, d_score, query_all, grad_all, sums,
):
    span, tokens, pair = window.shape
    head_dim = pair // 2
    width = queries.shape[1]
    reach = span * tokens
    both = HEAD_GROUP * tokens
    scale = 1.0 / math.sqrt(head_dim)
    shard, member = place[0], place[1]

    query_pos = shard * tokens + lax.broadcasted_iota(jnp.int32, (1, tokens), 1)
    first = jnp.zeros((1, tokens), jnp.int32)
    end = jnp.int32(0)
    for doc in range(2, place.shape[0]):
        end = end + place[doc]
        first = jnp.where(end <= query_pos, end, first)

    for slot in range(span):
        rows = pl.ds(slot * tokens, tokens)
        sender = (slot + MEMBER_FIRST) % span
        owner = shard - member + sender - jnp.where(sender > member, span, 0)
        key_pos = owner * tokens + lax.broadcasted_iota(jnp.int32, (tokens, tokens), 0)
        allowed = (key_pos >= first) & (key_pos <= query_pos)
        fill[rows, :] = jnp.where(allowed, 0.0, masked_fill)
        values = (window[slot, :, head_dim:].astype(f32) + bias[:, width:]).astype(bf16)
        value_rows[rows, :] = values
        value_cols[:, rows] = values.T
        key_cols[:, rows] = window[slot, :, :head_dim].T

    def scored(group):
        cols = [pl.ds((group * HEAD_GROUP + n) * head_dim, head_dim) for n in range(HEAD_GROUP)]
        query_rows = jnp.concatenate(
            [(queries[:, c].astype(f32) + bias[:, c]).astype(bf16) for c in cols], axis=0
        )
        grad_rows = jnp.concatenate([out_grad[:, c] for c in cols], axis=0)
        top = jnp.full((8, both), masked_fill, f32)
        for slot in range(span):
            rows = pl.ds(slot * tokens, tokens)
            part = transposed_product(window[slot, :, :head_dim], query_rows)
            part = part * (scale * math.log2(math.e)) + jnp.concatenate([fill[rows, :]] * 2, axis=1)
            score[group % 2, rows, :] = part
            top = jnp.maximum(top, jnp.max(part.reshape(tokens // 8, 8, both), axis=0))
        return query_rows, grad_rows, jnp.max(top, axis=0, keepdims=True)

    def finished(group, query_rows, grad_rows, top):
        here = pl.ds(group * both, both)
        total = jnp.zeros((8, both), f32)
        for slot in range(span):
            rows = pl.ds(slot * tokens, tokens)
            part = jnp.exp2(score[group % 2, rows, :] - top)
            total += jnp.sum(part.reshape(tokens // 8, 8, both), axis=0)
            power[rows, here] = part.astype(bf16)
        inverse = 1.0 / jnp.sum(total, axis=0, keepdims=True)
        found = jnp.dot(value_cols[...], power[:, here], preferred_element_type=f32) * inverse
        found = found.astype(bf16)
        grad_cols = grad_rows.T
        delta = jnp.sum(grad_cols.astype(f32) * found.astype(f32), axis=0, keepdims=True)
        for slot in range(span):
            rows = pl.ds(slot * tokens, tokens)
            d_probs = transposed_product(value_rows[rows, :], grad_rows)
            d_score[rows, here] = power[rows, here] * (d_probs - delta).astype(bf16)
        q_part = jnp.dot(key_cols[...], d_score[:, here], preferred_element_type=f32)
        q_part = (q_part * (inverse * scale)).T
        found = found.T
        column = jnp.broadcast_to(inverse, (head_dim, both)).T
        query_all[here, :] = (query_rows.astype(f32) * (column * scale)).astype(bf16)
        grad_all[here, :] = (grad_rows.astype(f32) * column).astype(bf16)
        for n in range(HEAD_GROUP):
            c = pl.ds((group * HEAD_GROUP + n) * head_dim, head_dim)
            rows = slice(n * tokens, (n + 1) * tokens)
            attended[:, c] = found[rows]
            q_grad[:, c] = q_part[rows]
            sums[group : group + 1, n * head_dim : (n + 1) * head_dim] = jnp.sum(
                q_part[rows], axis=0, keepdims=True
            )

    groups = width // (HEAD_GROUP * head_dim)
    ready = scored(0)
    for group in range(groups):
        following = scored(group + 1) if group + 1 < groups else None
        finished(group, *ready)
        ready = following

    value_sum = jnp.zeros((1, head_dim), f32)
    for slot in range(span):
        rows = pl.ds(slot * tokens, tokens)
        key_part = jnp.dot(d_score[rows, :], query_all[...], preferred_element_type=f32)
        value_part = jnp.dot(power[rows, :], grad_all[...], preferred_element_type=f32)
        partials[slot, :tokens, :head_dim] = key_part.astype(bf16)
        partials[slot, :tokens, head_dim:] = value_part.astype(bf16)
        value_sum += jnp.sum(value_part, axis=0, keepdims=True)
    sums[groups : groups + 1, :head_dim] = value_sum
    sums[groups : groups + 1, head_dim:] = jnp.zeros_like(value_sum)
    sums[groups + 1 :, :] = jnp.zeros((SUM_ROWS // 2 - groups - 1, pair), f32)
    high = sums[...].astype(bf16)
    low = (sums[...] - high.astype(f32)).astype(bf16)
    both_rows = jnp.concatenate([high, low], axis=0)
    for slot in range(span):
        partials[slot, tokens:, :] = both_rows


def attention(place, queries, out_grad, window, bias):
    tokens, width = queries.shape
    span, _, pair = window.shape
    head_dim = pair // 2
    reach = span * tokens
    vmem = pl.BlockSpec(memory_space=pltpu.VMEM)
    smem = pl.BlockSpec(memory_space=pltpu.SMEM)
    return pl.pallas_call(
        attention_kernel,
        out_shape=(
            jax.ShapeDtypeStruct((tokens, width), bf16),
            jax.ShapeDtypeStruct((tokens, width), f32),
            jax.ShapeDtypeStruct((span, tokens + SUM_ROWS, pair), bf16),
        ),
        in_specs=[smem] + [vmem] * 4,
        out_specs=(vmem,) * 3,
        scratch_shapes=[
            pltpu.VMEM((reach, head_dim), bf16),
            pltpu.VMEM((head_dim, reach), bf16),
            pltpu.VMEM((head_dim, reach), bf16),
            pltpu.VMEM((reach, tokens), f32),
            pltpu.VMEM((2, reach, HEAD_GROUP * tokens), f32),
            pltpu.VMEM((reach, width), bf16),
            pltpu.VMEM((reach, width), bf16),
            pltpu.VMEM((width, head_dim), bf16),
            pltpu.VMEM((width, head_dim), bf16),
            pltpu.VMEM((SUM_ROWS // 2, pair), f32),
        ],
        compiler_params=pltpu.CompilerParams(vmem_limit_bytes=40 * 1024 * 1024),
        cost_estimate=pl.CostEstimate(
            flops=12 * width * reach * tokens,
            bytes_accessed=4 * tokens * width * 2,
            transcendentals=reach * width,
        ),
        name="attention",
    )(place, queries, out_grad, window, bias)


def rotated(size, first):
    return [[(first + i) % size for i in range(size)]]


def exchanged(blocks, axis, first=0):
    return lax.all_to_all(
        blocks, axis, 0, 0, axis_index_groups=rotated(lax.axis_size(axis), first)
    )


def members_sum_kernel(received, copies):
    rows = jnp.sum(received[...].astype(f32), axis=0)
    rows = rows[: SUM_ROWS // 2] + rows[SUM_ROWS // 2 :]
    pair, width = received.shape[2], copies.shape[2]
    for start in range(0, width, pair):
        size = min(pair, width - start)
        part = rows[start // pair : start // pair + 1, :size]
        for copy in range(copies.shape[0]):
            copies[copy, :, start : start + size] = part


def members_sum(received, copies, width):
    span, rows, pair = received.shape
    return pl.pallas_call(
        members_sum_kernel,
        grid=(1,),
        out_shape=jax.ShapeDtypeStruct((copies, 1, width), f32),
        in_specs=[pl.BlockSpec((span, SUM_ROWS, pair), lambda i: (0, rows // SUM_ROWS - 1, 0))],
        out_specs=pl.BlockSpec((copies, 1, width), lambda i: (0, 0, 0)),
        name="members_sum",
    )(received)


def per_device(queries, keys, values, out_grad, q_bias, v_bias, doc_lengths):
    tokens, head_dim = keys.shape[1], keys.shape[2]
    width = queries.shape[2]
    groups = lax.axis_size("z") * lax.axis_size("y") // SPAN
    shard = lax.axis_index(SEQ)
    member = shard % SPAN
    place = jnp.concatenate([jnp.stack([shard, member]).astype(jnp.int32), doc_lengths[0]])
    bias = jnp.concatenate([q_bias, v_bias])[None]

    own = jnp.concatenate([keys[0], values[0]], axis=1)
    before = lax.ppermute(own, SEQ, [(i, i + SPAN) for i in range((groups - 1) * SPAN)])
    later = ((jnp.arange(SPAN) + MEMBER_FIRST) % SPAN >= member)[:, None, None]
    window = among_members(jnp.where(later, own[None], before[None]), groups)

    attended, q_grad, partials = attention(place, queries[0], out_grad[0], window, bias)

    received = among_members(partials, groups)
    copies = members_sum(received, lax.axis_size("rep"), width + head_dim)
    received = received[:, :tokens].astype(f32)
    mine = jnp.sum(jnp.where(later, received, 0.0), axis=0)
    others = jnp.sum(jnp.where(later, 0.0, received), axis=0).astype(bf16)
    returned = lax.ppermute(others, SEQ, [(i + SPAN, i) for i in range((groups - 1) * SPAN)])
    owned = mine + returned.astype(f32)

    rep_sums = jnp.sum(exchanged(copies, "rep"), axis=0)
    rep_sums, owned = lax.optimization_barrier((rep_sums, owned))
    copies = jnp.broadcast_to(rep_sums[None], (groups,) + rep_sums.shape)
    rows = along_groups(copies, groups)
    shards = groups * SPAN
    inverse = 1.0 / math.sqrt(shards * tokens * lax.axis_size("rep"))
    q_total = jnp.sum(rows[:, 0, :width], axis=0) * inverse
    v_total = jnp.sum(rows[:, 0, width:], axis=0) * inverse
    return (
        attended[None],
        q_grad[None],
        owned[None, :, :head_dim],
        owned[None, :, head_dim:],
        q_total,
        v_total,
    )


def among_members(blocks, groups):
    order = rotated(SPAN, MEMBER_FIRST)[0]
    return lax.all_to_all(
        blocks, SEQ, 0, 0, axis_index_groups=[[g * SPAN + m for m in order] for g in range(groups)]
    )


def along_groups(blocks, groups):
    order = rotated(groups, groups * LINE_FIRST // 8)[0]
    return lax.all_to_all(
        blocks, SEQ, 0, 0, axis_index_groups=[[g * SPAN + m for g in order] for m in range(SPAN)]
    )


def solution(mesh):
    seq, rep = mesh.shape["seq"], mesh.shape["rep"]
    fine = Mesh(mesh.devices.reshape(2 * seq // SPAN, SPAN // 2, rep), ("z", "y", "rep"))
    tokens = P("rep", SEQ, None)
    return jax.shard_map(
        per_device,
        mesh=fine,
        in_specs=(tokens, tokens, tokens, tokens, P(), P(), P("rep", None)),
        out_specs=(tokens, tokens, tokens, tokens, P(), P()),
        check_vma=False,
    )
```

```python
import functools
import math

import jax
import jax.numpy as jnp
from jax import lax
from jax.experimental import pallas as pl
from jax.experimental.pallas import tpu as pltpu
from jax.sharding import Mesh
from jax.sharding import PartitionSpec as P

SPAN = 8
HEAD_GROUP = 2
SEQ = ("z", "y")
MEMBER_FIRST = 7
LINE_FIRST = 5
REP_FIRST = 7
SUM_ROWS = 16
masked_fill = -1e30
f32 = jnp.float32
bf16 = jnp.bfloat16


def transposed_product(a, b):
    return lax.dot_general(a, b, (((1,), (1,)), ((), ())), preferred_element_type=f32)


def attention_kernel(
    place, queries, out_grad, window, bias,
    attended, q_grad, partials,
    value_rows, key_cols, value_cols, fill, score, power, d_score, query_all, grad_all, sums,
):
    span, tokens, pair = window.shape
    head_dim = pair // 2
    width = queries.shape[1]
    reach = span * tokens
    both = HEAD_GROUP * tokens
    scale = 1.0 / math.sqrt(head_dim)
    shard, member = place[0], place[1]

    query_pos = shard * tokens + lax.broadcasted_iota(jnp.int32, (1, tokens), 1)
    first = jnp.zeros((1, tokens), jnp.int32)
    end = jnp.int32(0)
    for doc in range(2, place.shape[0]):
        end = end + place[doc]
        first = jnp.where(end <= query_pos, end, first)

    for slot in range(span):
        rows = pl.ds(slot * tokens, tokens)
        sender = (slot + MEMBER_FIRST) % span
        owner = shard - member + sender - jnp.where(sender > member, span, 0)
        key_pos = owner * tokens + lax.broadcasted_iota(jnp.int32, (tokens, tokens), 0)
        allowed = (key_pos >= first) & (key_pos <= query_pos)
        fill[rows, :] = jnp.where(allowed, 0.0, masked_fill)
        values = (window[slot, :, head_dim:].astype(f32) + bias[:, width:]).astype(bf16)
        value_rows[rows, :] = values
        value_cols[:, rows] = values.T
        key_cols[:, rows] = window[slot, :, :head_dim].T

    def scored(group):
        cols = [pl.ds((group * HEAD_GROUP + n) * head_dim, head_dim) for n in range(HEAD_GROUP)]
        query_rows = jnp.concatenate(
            [(queries[:, c].astype(f32) + bias[:, c]).astype(bf16) for c in cols], axis=0
        )
        grad_rows = jnp.concatenate([out_grad[:, c] for c in cols], axis=0)
        top = jnp.full((8, both), masked_fill, f32)
        for slot in range(span):
            rows = pl.ds(slot * tokens, tokens)
            part = transposed_product(window[slot, :, :head_dim], query_rows)
            part = part * (scale * math.log2(math.e)) + jnp.concatenate([fill[rows, :]] * 2, axis=1)
            score[group % 2, rows, :] = part
            top = jnp.maximum(top, jnp.max(part.reshape(tokens // 8, 8, both), axis=0))
        return query_rows, grad_rows, jnp.max(top, axis=0, keepdims=True)

    def finished(group, query_rows, grad_rows, top):
        here = pl.ds(group * both, both)
        total = jnp.zeros((8, both), f32)
        for slot in range(span):
            rows = pl.ds(slot * tokens, tokens)
            part = jnp.exp2(score[group % 2, rows, :] - top)
            total += jnp.sum(part.reshape(tokens // 8, 8, both), axis=0)
            power[rows, here] = part.astype(bf16)
        inverse = 1.0 / jnp.sum(total, axis=0, keepdims=True)
        found = jnp.dot(value_cols[...], power[:, here], preferred_element_type=f32) * inverse
        found = found.astype(bf16)
        grad_cols = grad_rows.T
        delta = jnp.sum(grad_cols.astype(f32) * found.astype(f32), axis=0, keepdims=True)
        for slot in range(span):
            rows = pl.ds(slot * tokens, tokens)
            d_probs = transposed_product(value_rows[rows, :], grad_rows)
            d_score[rows, here] = power[rows, here] * (d_probs - delta).astype(bf16)
        q_part = jnp.dot(key_cols[...], d_score[:, here], preferred_element_type=f32)
        q_part = (q_part * (inverse * scale)).T
        found = found.T
        column = jnp.broadcast_to(inverse, (head_dim, both)).T
        query_all[here, :] = (query_rows.astype(f32) * (column * scale)).astype(bf16)
        grad_all[here, :] = (grad_rows.astype(f32) * column).astype(bf16)
        for n in range(HEAD_GROUP):
            c = pl.ds((group * HEAD_GROUP + n) * head_dim, head_dim)
            rows = slice(n * tokens, (n + 1) * tokens)
            attended[:, c] = found[rows]
            q_grad[:, c] = q_part[rows]
            sums[group : group + 1, n * head_dim : (n + 1) * head_dim] = jnp.sum(
                q_part[rows], axis=0, keepdims=True
            )

    groups = width // (HEAD_GROUP * head_dim)
    ready = scored(0)
    for group in range(groups):
        following = scored(group + 1) if group + 1 < groups else None
        finished(group, *ready)
        ready = following

    value_sum = jnp.zeros((1, head_dim), f32)
    for slot in range(span):
        rows = pl.ds(slot * tokens, tokens)
        key_part = jnp.dot(d_score[rows, :], query_all[...], preferred_element_type=f32)
        value_part = jnp.dot(power[rows, :], grad_all[...], preferred_element_type=f32)
        partials[slot, :tokens, :head_dim] = key_part.astype(bf16)
        partials[slot, :tokens, head_dim:] = value_part.astype(bf16)
        value_sum += jnp.sum(value_part, axis=0, keepdims=True)
    sums[groups : groups + 1, :head_dim] = value_sum
    sums[groups : groups + 1, head_dim:] = jnp.zeros_like(value_sum)
    sums[groups + 1 :, :] = jnp.zeros((SUM_ROWS // 2 - groups - 1, pair), f32)
    high = sums[...].astype(bf16)
    low = (sums[...] - high.astype(f32)).astype(bf16)
    both_rows = jnp.concatenate([high, low], axis=0)
    for slot in range(span):
        partials[slot, tokens:, :] = both_rows


def attention(place, queries, out_grad, window, bias):
    tokens, width = queries.shape
    span, _, pair = window.shape
    head_dim = pair // 2
    reach = span * tokens
    vmem = pl.BlockSpec(memory_space=pltpu.VMEM)
    smem = pl.BlockSpec(memory_space=pltpu.SMEM)
    return pl.pallas_call(
        attention_kernel,
        out_shape=(
            jax.ShapeDtypeStruct((tokens, width), bf16),
            jax.ShapeDtypeStruct((tokens, width), f32),
            jax.ShapeDtypeStruct((span, tokens + SUM_ROWS, pair), bf16),
        ),
        in_specs=[smem] + [vmem] * 4,
        out_specs=(vmem,) * 3,
        scratch_shapes=[
            pltpu.VMEM((reach, head_dim), bf16),
            pltpu.VMEM((head_dim, reach), bf16),
            pltpu.VMEM((head_dim, reach), bf16),
            pltpu.VMEM((reach, tokens), f32),
            pltpu.VMEM((2, reach, HEAD_GROUP * tokens), f32),
            pltpu.VMEM((reach, width), bf16),
            pltpu.VMEM((reach, width), bf16),
            pltpu.VMEM((width, head_dim), bf16),
            pltpu.VMEM((width, head_dim), bf16),
            pltpu.VMEM((SUM_ROWS // 2, pair), f32),
        ],
        compiler_params=pltpu.CompilerParams(vmem_limit_bytes=40 * 1024 * 1024),
        cost_estimate=pl.CostEstimate(
            flops=12 * width * reach * tokens,
            bytes_accessed=4 * tokens * width * 2,
            transcendentals=reach * width,
        ),
        name="attention",
    )(place, queries, out_grad, window, bias)


def rotated(size, first):
    return [[(first + i) % size for i in range(size)]]


def exchanged(blocks, axis, first=0):
    return lax.all_to_all(
        blocks, axis, 0, 0, axis_index_groups=rotated(lax.axis_size(axis), first)
    )


def per_device(queries, keys, values, out_grad, q_bias, v_bias, doc_lengths):
    tokens, head_dim = keys.shape[1], keys.shape[2]
    width = queries.shape[2]
    groups = lax.axis_size("z") * lax.axis_size("y") // SPAN
    shard = lax.axis_index(SEQ)
    member = shard % SPAN
    place = jnp.concatenate([jnp.stack([shard, member]).astype(jnp.int32), doc_lengths[0]])
    bias = jnp.concatenate([q_bias, v_bias])[None]

    own = jnp.concatenate([keys[0], values[0]], axis=1)
    before = lax.ppermute(own, SEQ, [(i, i + SPAN) for i in range((groups - 1) * SPAN)])
    later = ((jnp.arange(SPAN) + MEMBER_FIRST) % SPAN >= member)[:, None, None]
    before, place, bias = lax.optimization_barrier((before, place, bias))
    window = among_members(jnp.where(later, own[None], before[None]), groups)

    attended, q_grad, partials = attention(place, queries[0], out_grad[0], window, bias)

    received = among_members(partials, groups)
    sums = jnp.sum(received[:, tokens:].astype(f32), axis=0)
    sums = sums[: SUM_ROWS // 2] + sums[SUM_ROWS // 2 :]
    copies = jnp.broadcast_to(sums[None], (lax.axis_size("rep"),) + sums.shape)
    received = received[:, :tokens].astype(f32)
    mine = jnp.sum(jnp.where(later, received, 0.0), axis=0)
    others = jnp.sum(jnp.where(later, 0.0, received), axis=0).astype(bf16)
    returned = lax.ppermute(others, SEQ, [(i + SPAN, i) for i in range((groups - 1) * SPAN)])
    owned = mine + returned.astype(f32)

    rep_sums = jnp.sum(exchanged(copies, "rep", REP_FIRST), axis=0)
    k_grad, v_grad = owned[None, :, :head_dim], owned[None, :, head_dim:]
    rep_sums, k_grad, v_grad = lax.optimization_barrier((rep_sums, k_grad, v_grad))
    copies = jnp.broadcast_to(rep_sums[None], (groups,) + rep_sums.shape)
    rows = along_groups(copies, groups)
    shards = groups * SPAN
    inverse = 1.0 / math.sqrt(shards * tokens * lax.axis_size("rep"))
    totals = jnp.sum(rows, axis=0) * inverse
    full = width // (2 * head_dim)
    q_total = totals[:full].reshape(width)
    v_total = totals[full, :head_dim]
    return (
        attended[None],
        q_grad[None],
        k_grad,
        v_grad,
        q_total,
        v_total,
    )


def among_members(blocks, groups):
    order = rotated(SPAN, MEMBER_FIRST)[0]
    return lax.all_to_all(
        blocks, SEQ, 0, 0, axis_index_groups=[[g * SPAN + m for m in order] for g in range(groups)]
    )


def along_groups(blocks, groups):
    order = rotated(groups, groups * LINE_FIRST // 8)[0]
    return lax.all_to_all(
        blocks, SEQ, 0, 0, axis_index_groups=[[g * SPAN + m for g in order] for m in range(SPAN)]
    )


def solution(mesh):
    seq, rep = mesh.shape["seq"], mesh.shape["rep"]
    fine = Mesh(mesh.devices.reshape(2 * seq // SPAN, SPAN // 2, rep), ("z", "y", "rep"))
    tokens = P("rep", SEQ, None)
    return jax.shard_map(
        per_device,
        mesh=fine,
        in_specs=(tokens, tokens, tokens, tokens, P(), P(), P("rep", None)),
        out_specs=(tokens, tokens, tokens, tokens, P(), P()),
        check_vma=False,
    )
```

```python
import functools
import math

import jax
import jax.numpy as jnp
from jax import lax
from jax.experimental import pallas as pl
from jax.experimental.pallas import tpu as pltpu
from jax.sharding import Mesh
from jax.sharding import PartitionSpec as P

SPAN = 8
HEAD_GROUP = 4
SEQ = ("z", "y")
MEMBER_FIRST = 7
LINE_FIRST = 5
REP_FIRST = 7
SUM_ROWS = 16
masked_fill = -1e30
f32 = jnp.float32
bf16 = jnp.bfloat16


def transposed_product(a, b):
    return lax.dot_general(a, b, (((1,), (1,)), ((), ())), preferred_element_type=f32)


def attention_kernel(
    place, queries, out_grad, window, bias,
    attended, q_grad, partials,
    value_rows, key_cols, value_cols, fill, score, power, d_score, query_all, grad_all, sums,
):
    span, tokens, pair = window.shape
    head_dim = pair // 2
    width = queries.shape[1]
    reach = span * tokens
    both = HEAD_GROUP * tokens
    scale = 1.0 / math.sqrt(head_dim)
    shard, member = place[0], place[1]

    query_pos = shard * tokens + lax.broadcasted_iota(jnp.int32, (1, tokens), 1)
    first = jnp.zeros((1, tokens), jnp.int32)
    end = jnp.int32(0)
    for doc in range(2, place.shape[0]):
        end = end + place[doc]
        first = jnp.where(end <= query_pos, end, first)

    for slot in range(span):
        rows = pl.ds(slot * tokens, tokens)
        sender = (slot + MEMBER_FIRST) % span
        owner = shard - member + sender - jnp.where(sender > member, span, 0)
        key_pos = owner * tokens + lax.broadcasted_iota(jnp.int32, (tokens, tokens), 0)
        allowed = (key_pos >= first) & (key_pos <= query_pos)
        fill[rows, :] = jnp.where(allowed, 0.0, masked_fill)
        values = (window[slot, :, head_dim:].astype(f32) + bias[:, width:]).astype(bf16)
        value_rows[rows, :] = values
        value_cols[:, rows] = values.T
        key_cols[:, rows] = window[slot, :, :head_dim].T

    def scored(group):
        cols = [pl.ds((group * HEAD_GROUP + n) * head_dim, head_dim) for n in range(HEAD_GROUP)]
        query_rows = jnp.concatenate(
            [(queries[:, c].astype(f32) + bias[:, c]).astype(bf16) for c in cols], axis=0
        )
        grad_rows = jnp.concatenate([out_grad[:, c] for c in cols], axis=0)
        top = jnp.full((8, both), masked_fill, f32)
        for slot in range(span):
            rows = pl.ds(slot * tokens, tokens)
            part = transposed_product(window[slot, :, :head_dim], query_rows)
            part = part * (scale * math.log2(math.e)) + jnp.concatenate([fill[rows, :]] * HEAD_GROUP, axis=1)
            score[group % 2, rows, :] = part
            top = jnp.maximum(top, jnp.max(part.reshape(tokens // 8, 8, both), axis=0))
        return query_rows, grad_rows, jnp.max(top, axis=0, keepdims=True)

    def finished(group, query_rows, grad_rows, top):
        here = pl.ds(group * both, both)
        total = jnp.zeros((8, both), f32)
        for slot in range(span):
            rows = pl.ds(slot * tokens, tokens)
            part = jnp.exp2(score[group % 2, rows, :] - top)
            total += jnp.sum(part.reshape(tokens // 8, 8, both), axis=0)
            power[rows, here] = part.astype(bf16)
        inverse = 1.0 / jnp.sum(total, axis=0, keepdims=True)
        found = jnp.dot(value_cols[...], power[:, here], preferred_element_type=f32) * inverse
        found = found.astype(bf16)
        grad_cols = grad_rows.T
        delta = jnp.sum(grad_cols.astype(f32) * found.astype(f32), axis=0, keepdims=True)
        for slot in range(span):
            rows = pl.ds(slot * tokens, tokens)
            d_probs = transposed_product(value_rows[rows, :], grad_rows)
            d_score[rows, here] = power[rows, here] * (d_probs - delta).astype(bf16)
        q_part = jnp.dot(key_cols[...], d_score[:, here], preferred_element_type=f32)
        q_part = (q_part * (inverse * scale)).T
        found = found.T
        column = jnp.broadcast_to(inverse, (head_dim, both)).T
        query_all[here, :] = (query_rows.astype(f32) * (column * scale)).astype(bf16)
        grad_all[here, :] = (grad_rows.astype(f32) * column).astype(bf16)
        for n in range(HEAD_GROUP):
            c = pl.ds((group * HEAD_GROUP + n) * head_dim, head_dim)
            rows = slice(n * tokens, (n + 1) * tokens)
            attended[:, c] = found[rows]
            q_grad[:, c] = q_part[rows]
            head = group * HEAD_GROUP + n
            sums[head // 2 : head // 2 + 1, head % 2 * head_dim : (head % 2 + 1) * head_dim] = (
                jnp.sum(q_part[rows], axis=0, keepdims=True)
            )

    groups = width // (HEAD_GROUP * head_dim)
    ready = scored(0)
    for group in range(groups):
        following = scored(group + 1) if group + 1 < groups else None
        finished(group, *ready)
        ready = following

    value_sum = jnp.zeros((1, head_dim), f32)
    for slot in range(span):
        rows = pl.ds(slot * tokens, tokens)
        key_part = jnp.dot(d_score[rows, :], query_all[...], preferred_element_type=f32)
        value_part = jnp.dot(power[rows, :], grad_all[...], preferred_element_type=f32)
        partials[slot, :tokens, :head_dim] = key_part.astype(bf16)
        partials[slot, :tokens, head_dim:] = value_part.astype(bf16)
        value_sum += jnp.sum(value_part, axis=0, keepdims=True)
    full = width // pair
    sums[full : full + 1, :head_dim] = value_sum
    sums[full : full + 1, head_dim:] = jnp.zeros_like(value_sum)
    sums[full + 1 :, :] = jnp.zeros((SUM_ROWS // 2 - full - 1, pair), f32)
    high = sums[...].astype(bf16)
    low = (sums[...] - high.astype(f32)).astype(bf16)
    both_rows = jnp.concatenate([high, low], axis=0)
    for slot in range(span):
        partials[slot, tokens:, :] = both_rows


def attention(place, queries, out_grad, window, bias):
    tokens, width = queries.shape
    span, _, pair = window.shape
    head_dim = pair // 2
    reach = span * tokens
    vmem = pl.BlockSpec(memory_space=pltpu.VMEM)
    smem = pl.BlockSpec(memory_space=pltpu.SMEM)
    return pl.pallas_call(
        attention_kernel,
        out_shape=(
            jax.ShapeDtypeStruct((tokens, width), bf16),
            jax.ShapeDtypeStruct((tokens, width), f32),
            jax.ShapeDtypeStruct((span, tokens + SUM_ROWS, pair), bf16),
        ),
        in_specs=[smem] + [vmem] * 4,
        out_specs=(vmem,) * 3,
        scratch_shapes=[
            pltpu.VMEM((reach, head_dim), bf16),
            pltpu.VMEM((head_dim, reach), bf16),
            pltpu.VMEM((head_dim, reach), bf16),
            pltpu.VMEM((reach, tokens), f32),
            pltpu.VMEM((2, reach, HEAD_GROUP * tokens), f32),
            pltpu.VMEM((reach, width), bf16),
            pltpu.VMEM((reach, width), bf16),
            pltpu.VMEM((width, head_dim), bf16),
            pltpu.VMEM((width, head_dim), bf16),
            pltpu.VMEM((SUM_ROWS // 2, pair), f32),
        ],
        compiler_params=pltpu.CompilerParams(vmem_limit_bytes=40 * 1024 * 1024),
        cost_estimate=pl.CostEstimate(
            flops=12 * width * reach * tokens,
            bytes_accessed=4 * tokens * width * 2,
            transcendentals=reach * width,
        ),
        name="attention",
    )(place, queries, out_grad, window, bias)


def rotated(size, first):
    return [[(first + i) % size for i in range(size)]]


def exchanged(blocks, axis, first=0):
    return lax.all_to_all(
        blocks, axis, 0, 0, axis_index_groups=rotated(lax.axis_size(axis), first)
    )


def per_device(queries, keys, values, out_grad, q_bias, v_bias, doc_lengths):
    tokens, head_dim = keys.shape[1], keys.shape[2]
    width = queries.shape[2]
    groups = lax.axis_size("z") * lax.axis_size("y") // SPAN
    shard = lax.axis_index(SEQ)
    member = shard % SPAN
    place = jnp.concatenate([jnp.stack([shard, member]).astype(jnp.int32), doc_lengths[0]])
    bias = jnp.concatenate([q_bias, v_bias])[None]

    own = jnp.concatenate([keys[0], values[0]], axis=1)
    before = lax.ppermute(own, SEQ, [(i, i + SPAN) for i in range((groups - 1) * SPAN)])
    later = ((jnp.arange(SPAN) + MEMBER_FIRST) % SPAN >= member)[:, None, None]
    before, place, bias = lax.optimization_barrier((before, place, bias))
    window = among_members(jnp.where(later, own[None], before[None]), groups)

    attended, q_grad, partials = attention(place, queries[0], out_grad[0], window, bias)

    received = among_members(partials, groups)
    sums = jnp.sum(received[:, tokens:].astype(f32), axis=0)
    sums = sums[: SUM_ROWS // 2] + sums[SUM_ROWS // 2 :]
    full = width // (2 * head_dim)
    sums = jnp.concatenate([sums[:full], sums[full : 2 * full, :head_dim]], axis=1)
    copies = jnp.broadcast_to(sums[None], (lax.axis_size("rep"),) + sums.shape)
    received = received[:, :tokens].astype(f32)
    mine = jnp.sum(jnp.where(later, received, 0.0), axis=0)
    others = jnp.sum(jnp.where(later, 0.0, received), axis=0).astype(bf16)
    returned = lax.ppermute(others, SEQ, [(i + SPAN, i) for i in range((groups - 1) * SPAN)])

    rep_sums = jnp.sum(exchanged(copies, "rep", REP_FIRST), axis=0)
    k_grad = mine[None, :, :head_dim] + returned[None, :, :head_dim].astype(f32)
    v_grad = mine[None, :, head_dim:] + returned[None, :, head_dim:].astype(f32)
    rep_sums, k_grad, v_grad = lax.optimization_barrier((rep_sums, k_grad, v_grad))
    copies = jnp.broadcast_to(rep_sums[None], (groups,) + rep_sums.shape)
    rows = along_groups(copies, groups)
    shards = groups * SPAN
    inverse = 1.0 / math.sqrt(shards * tokens * lax.axis_size("rep"))
    totals = jnp.sum(rows, axis=0) * inverse
    q_total = totals[:, : 2 * head_dim].reshape(width)
    v_total = totals[0, 2 * head_dim :]
    return (
        attended[None],
        q_grad[None],
        k_grad,
        v_grad,
        q_total,
        v_total,
    )


def among_members(blocks, groups):
    order = rotated(SPAN, MEMBER_FIRST)[0]
    return lax.all_to_all(
        blocks, SEQ, 0, 0, axis_index_groups=[[g * SPAN + m for m in order] for g in range(groups)]
    )


def along_groups(blocks, groups):
    order = rotated(groups, groups * LINE_FIRST // 8)[0]
    return lax.all_to_all(
        blocks, SEQ, 0, 0, axis_index_groups=[[g * SPAN + m for g in order] for m in range(SPAN)]
    )


def solution(mesh):
    seq, rep = mesh.shape["seq"], mesh.shape["rep"]
    fine = Mesh(mesh.devices.reshape(2 * seq // SPAN, SPAN // 2, rep), ("z", "y", "rep"))
    tokens = P("rep", SEQ, None)
    return jax.shard_map(
        per_device,
        mesh=fine,
        in_specs=(tokens, tokens, tokens, tokens, P(), P(), P("rep", None)),
        out_specs=(tokens, tokens, tokens, tokens, P(), P()),
        check_vma=False,
    )
```

```python
import functools
import math

import jax
import jax.numpy as jnp
from jax import lax
from jax.experimental import pallas as pl
from jax.experimental.pallas import tpu as pltpu
from jax.sharding import Mesh
from jax.sharding import PartitionSpec as P

SPAN = 8
HEAD_GROUP = 4
SEQ = ("z", "y")
MEMBER_FIRST = 7
LINE_FIRST = 5
REP_FIRST = 7
SUM_ROWS = 16
masked_fill = -1e30
f32 = jnp.float32
bf16 = jnp.bfloat16


def transposed_product(a, b):
    return lax.dot_general(a, b, (((1,), (1,)), ((), ())), preferred_element_type=f32)


def attention_kernel(
    place, queries, out_grad, window, bias,
    attended, q_grad, partials,
    value_rows, key_cols, value_cols, fill, score, power, d_score, query_all, grad_all, sums,
):
    span, tokens, pair = window.shape
    head_dim = pair // 2
    width = queries.shape[1]
    reach = span * tokens
    both = HEAD_GROUP * tokens
    scale = 1.0 / math.sqrt(head_dim)
    shard, member = place[0], place[1]

    query_pos = shard * tokens + lax.broadcasted_iota(jnp.int32, (1, tokens), 1)
    first = jnp.zeros((1, tokens), jnp.int32)
    end = jnp.int32(0)
    for doc in range(2, place.shape[0]):
        end = end + place[doc]
        first = jnp.where(end <= query_pos, end, first)

    for slot in range(span):
        rows = pl.ds(slot * tokens, tokens)
        sender = (slot + MEMBER_FIRST) % span
        owner = shard - member + sender - jnp.where(sender > member, span, 0)
        key_pos = owner * tokens + lax.broadcasted_iota(jnp.int32, (tokens, tokens), 0)
        allowed = (key_pos >= first) & (key_pos <= query_pos)
        fill[rows, :] = jnp.where(allowed, 0.0, masked_fill)
        values = (window[slot, :, head_dim:].astype(f32) + bias[:, width:]).astype(bf16)
        value_rows[rows, :] = values
        value_cols[:, rows] = values.T
        key_cols[:, rows] = window[slot, :, :head_dim].T

    def scored(group):
        cols = [pl.ds((group * HEAD_GROUP + n) * head_dim, head_dim) for n in range(HEAD_GROUP)]
        query_rows = jnp.concatenate(
            [(queries[:, c].astype(f32) + bias[:, c]).astype(bf16) for c in cols], axis=0
        )
        grad_rows = jnp.concatenate([out_grad[:, c] for c in cols], axis=0)
        top = jnp.full((8, both), masked_fill, f32)
        for slot in range(span):
            rows = pl.ds(slot * tokens, tokens)
            part = transposed_product(window[slot, :, :head_dim], query_rows)
            part = part * (scale * math.log2(math.e)) + jnp.concatenate([fill[rows, :]] * HEAD_GROUP, axis=1)
            score[group % 2, rows, :] = part
            top = jnp.maximum(top, jnp.max(part.reshape(tokens // 8, 8, both), axis=0))
        return query_rows, grad_rows, jnp.max(top, axis=0, keepdims=True)

    def finished(group, query_rows, grad_rows, top):
        here = pl.ds(group * both, both)
        total = jnp.zeros((8, both), f32)
        for slot in range(span):
            rows = pl.ds(slot * tokens, tokens)
            part = jnp.exp2(score[group % 2, rows, :] - top)
            total += jnp.sum(part.reshape(tokens // 8, 8, both), axis=0)
            power[rows, here] = part.astype(bf16)
        inverse = 1.0 / jnp.sum(total, axis=0, keepdims=True)
        found = jnp.dot(value_cols[...], power[:, here], preferred_element_type=f32) * inverse
        found = found.astype(bf16)
        grad_cols = grad_rows.T
        delta = jnp.sum(grad_cols.astype(f32) * found.astype(f32), axis=0, keepdims=True)
        for slot in range(span):
            rows = pl.ds(slot * tokens, tokens)
            d_probs = transposed_product(value_rows[rows, :], grad_rows)
            d_score[rows, here] = power[rows, here] * (d_probs - delta).astype(bf16)
        q_part = jnp.dot(key_cols[...], d_score[:, here], preferred_element_type=f32)
        q_part = (q_part * (inverse * scale)).T
        found = found.T
        column = jnp.broadcast_to(inverse, (head_dim, both)).T
        query_all[here, :] = (query_rows.astype(f32) * (column * scale)).astype(bf16)
        grad_all[here, :] = (grad_rows.astype(f32) * column).astype(bf16)
        for n in range(HEAD_GROUP):
            c = pl.ds((group * HEAD_GROUP + n) * head_dim, head_dim)
            rows = slice(n * tokens, (n + 1) * tokens)
            attended[:, c] = found[rows]
            q_grad[:, c] = q_part[rows]
            head = group * HEAD_GROUP + n
            sums[head // 2 : head // 2 + 1, head % 2 * head_dim : (head % 2 + 1) * head_dim] = (
                jnp.sum(q_part[rows], axis=0, keepdims=True)
            )

    groups = width // (HEAD_GROUP * head_dim)
    ready = scored(0)
    for group in range(groups):
        following = scored(group + 1) if group + 1 < groups else None
        finished(group, *ready)
        ready = following

    value_sum = jnp.zeros((1, head_dim), f32)
    for slot in range(span):
        rows = pl.ds(slot * tokens, tokens)
        key_part = jnp.dot(d_score[rows, :], query_all[...], preferred_element_type=f32)
        value_part = jnp.dot(power[rows, :], grad_all[...], preferred_element_type=f32)
        partials[slot, :tokens, :head_dim] = key_part.astype(bf16)
        partials[slot, :tokens, head_dim:] = value_part.astype(bf16)
        value_sum += jnp.sum(value_part, axis=0, keepdims=True)
    full = width // pair
    sums[full : full + 1, :head_dim] = value_sum
    sums[full : full + 1, head_dim:] = jnp.zeros_like(value_sum)
    sums[full + 1 :, :] = jnp.zeros((SUM_ROWS // 2 - full - 1, pair), f32)
    high = sums[...].astype(bf16)
    low = (sums[...] - high.astype(f32)).astype(bf16)
    both_rows = jnp.concatenate([high, low], axis=0)
    for slot in range(span):
        partials[slot, tokens:, :] = both_rows


def attention(place, queries, out_grad, window, bias):
    tokens, width = queries.shape
    span, _, pair = window.shape
    head_dim = pair // 2
    reach = span * tokens
    vmem = pl.BlockSpec(memory_space=pltpu.VMEM)
    smem = pl.BlockSpec(memory_space=pltpu.SMEM)
    return pl.pallas_call(
        attention_kernel,
        out_shape=(
            jax.ShapeDtypeStruct((tokens, width), bf16),
            jax.ShapeDtypeStruct((tokens, width), f32),
            jax.ShapeDtypeStruct((span, tokens + SUM_ROWS, pair), bf16),
        ),
        in_specs=[smem] + [vmem] * 4,
        out_specs=(vmem,) * 3,
        scratch_shapes=[
            pltpu.VMEM((reach, head_dim), bf16),
            pltpu.VMEM((head_dim, reach), bf16),
            pltpu.VMEM((head_dim, reach), bf16),
            pltpu.VMEM((reach, tokens), f32),
            pltpu.VMEM((2, reach, HEAD_GROUP * tokens), f32),
            pltpu.VMEM((reach, width), bf16),
            pltpu.VMEM((reach, width), bf16),
            pltpu.VMEM((width, head_dim), bf16),
            pltpu.VMEM((width, head_dim), bf16),
            pltpu.VMEM((SUM_ROWS // 2, pair), f32),
        ],
        compiler_params=pltpu.CompilerParams(vmem_limit_bytes=40 * 1024 * 1024),
        cost_estimate=pl.CostEstimate(
            flops=12 * width * reach * tokens,
            bytes_accessed=4 * tokens * width * 2,
            transcendentals=reach * width,
        ),
        name="attention",
    )(place, queries, out_grad, window, bias)


def rotated(size, first):
    return [[(first + i) % size for i in range(size)]]


def exchanged(blocks, axis, first=0):
    return lax.all_to_all(
        blocks, axis, 0, 0, axis_index_groups=rotated(lax.axis_size(axis), first)
    )


def per_device(queries, keys, values, out_grad, q_bias, v_bias, doc_lengths):
    tokens, head_dim = keys.shape[1], keys.shape[2]
    width = queries.shape[2]
    groups = lax.axis_size("z") * lax.axis_size("y") // SPAN
    shard = lax.axis_index(SEQ)
    member = shard % SPAN
    place = jnp.concatenate([jnp.stack([shard, member]).astype(jnp.int32), doc_lengths[0]])
    bias = jnp.concatenate([q_bias, v_bias])[None]

    own = jnp.concatenate([keys[0], values[0]], axis=1)
    before = lax.ppermute(own, SEQ, [(i, i + SPAN) for i in range((groups - 1) * SPAN)])
    later = ((jnp.arange(SPAN) + MEMBER_FIRST) % SPAN >= member)[:, None, None]
    before, place, bias = lax.optimization_barrier((before, place, bias))
    window = among_members(jnp.where(later, own[None], before[None]), groups)

    attended, q_grad, partials = attention(place, queries[0], out_grad[0], window, bias)

    received = among_members(partials, groups)
    inverse = 1.0 / math.sqrt(groups * SPAN * tokens * lax.axis_size("rep"))
    sums = jnp.sum(received[:, tokens:].astype(f32), axis=0) * inverse
    sums = sums[: SUM_ROWS // 2] + sums[SUM_ROWS // 2 :]
    full = width // (2 * head_dim)
    sums = jnp.concatenate([sums[:full], sums[full : 2 * full, :head_dim]], axis=1)
    copies = jnp.broadcast_to(sums[None], (lax.axis_size("rep"),) + sums.shape)
    received = received[:, :tokens].astype(f32)
    mine = jnp.sum(jnp.where(later, received, 0.0), axis=0)
    others = jnp.sum(jnp.where(later, 0.0, received), axis=0).astype(bf16)
    returned = lax.ppermute(others, SEQ, [(i + SPAN, i) for i in range((groups - 1) * SPAN)])

    rep_sums = jnp.sum(exchanged(copies, "rep", REP_FIRST), axis=0)
    k_grad = mine[None, :, :head_dim] + returned[None, :, :head_dim].astype(f32)
    v_grad = mine[None, :, head_dim:] + returned[None, :, head_dim:].astype(f32)
    rep_sums, k_grad, v_grad = lax.optimization_barrier((rep_sums, k_grad, v_grad))
    copies = jnp.broadcast_to(rep_sums[None], (groups,) + rep_sums.shape)
    rows = along_groups(copies, groups)
    q_total = jnp.sum(rows[:, :, : 2 * head_dim], axis=0).reshape(width)
    v_total = jnp.sum(rows[:, 0, 2 * head_dim :], axis=0)
    return (
        attended[None],
        q_grad[None],
        k_grad,
        v_grad,
        q_total,
        v_total,
    )


def among_members(blocks, groups):
    order = rotated(SPAN, MEMBER_FIRST)[0]
    return lax.all_to_all(
        blocks, SEQ, 0, 0, axis_index_groups=[[g * SPAN + m for m in order] for g in range(groups)]
    )


def along_groups(blocks, groups):
    order = rotated(groups, groups * LINE_FIRST // 8)[0]
    return lax.all_to_all(
        blocks, SEQ, 0, 0, axis_index_groups=[[g * SPAN + m for g in order] for m in range(SPAN)]
    )


def solution(mesh):
    seq, rep = mesh.shape["seq"], mesh.shape["rep"]
    fine = Mesh(mesh.devices.reshape(2 * seq // SPAN, SPAN // 2, rep), ("z", "y", "rep"))
    tokens = P("rep", SEQ, None)
    return jax.shard_map(
        per_device,
        mesh=fine,
        in_specs=(tokens, tokens, tokens, tokens, P(), P(), P("rep", None)),
        out_specs=(tokens, tokens, tokens, tokens, P(), P()),
        check_vma=False,
    )
```

```python
import functools
import math

import jax
import jax.numpy as jnp
from jax import lax
from jax.experimental import pallas as pl
from jax.experimental.pallas import tpu as pltpu
from jax.sharding import Mesh
from jax.sharding import PartitionSpec as P

SPAN = 8
HEAD_GROUP = 4
SEQ = ("z", "y")
MEMBER_FIRST = 7
LINE_FIRST = 5
REP_FIRST = 7
SUM_ROWS = 16
masked_fill = -1e30
f32 = jnp.float32
bf16 = jnp.bfloat16


def transposed_product(a, b):
    return lax.dot_general(a, b, (((1,), (1,)), ((), ())), preferred_element_type=f32)


def attention_kernel(
    place, queries, out_grad, window, bias,
    attended, q_grad, partials,
    value_rows, key_cols, value_cols, fill, score, power, d_score, query_all, grad_all, sums,
):
    span, tokens, pair = window.shape
    head_dim = pair // 2
    width = queries.shape[1]
    reach = span * tokens
    both = HEAD_GROUP * tokens
    scale = 1.0 / math.sqrt(head_dim)
    shard, member = place[0], place[1]

    query_pos = shard * tokens + lax.broadcasted_iota(jnp.int32, (1, tokens), 1)
    first = jnp.zeros((1, tokens), jnp.int32)
    end = jnp.int32(0)
    for doc in range(2, place.shape[0]):
        end = end + place[doc]
        first = jnp.where(end <= query_pos, end, first)

    for slot in range(span):
        rows = pl.ds(slot * tokens, tokens)
        sender = (slot + MEMBER_FIRST) % span
        owner = shard - member + sender - jnp.where(sender > member, span, 0)
        key_pos = owner * tokens + lax.broadcasted_iota(jnp.int32, (tokens, tokens), 0)
        allowed = (key_pos >= first) & (key_pos <= query_pos)
        fill[rows, :] = jnp.where(allowed, 0.0, masked_fill)
        values = (window[slot, :, head_dim:].astype(f32) + bias[:, width:]).astype(bf16)
        value_rows[rows, :] = values
        value_cols[:, rows] = values.T
        key_cols[:, rows] = window[slot, :, :head_dim].T

    def scored(group):
        cols = [pl.ds((group * HEAD_GROUP + n) * head_dim, head_dim) for n in range(HEAD_GROUP)]
        query_rows = jnp.concatenate(
            [(queries[:, c].astype(f32) + bias[:, c]).astype(bf16) for c in cols], axis=0
        )
        grad_rows = jnp.concatenate([out_grad[:, c] for c in cols], axis=0)
        top = jnp.full((8, both), masked_fill, f32)
        for slot in range(span):
            rows = pl.ds(slot * tokens, tokens)
            part = transposed_product(window[slot, :, :head_dim], query_rows)
            part = part * (scale * math.log2(math.e)) + jnp.concatenate([fill[rows, :]] * HEAD_GROUP, axis=1)
            score[group % 2, rows, :] = part
            top = jnp.maximum(top, jnp.max(part.reshape(tokens // 8, 8, both), axis=0))
        return query_rows, grad_rows, jnp.max(top, axis=0, keepdims=True)

    def finished(group, query_rows, grad_rows, top):
        here = pl.ds(group * both, both)
        total = jnp.zeros((8, both), f32)
        for slot in range(span):
            rows = pl.ds(slot * tokens, tokens)
            part = jnp.exp2(score[group % 2, rows, :] - top)
            total += jnp.sum(part.reshape(tokens // 8, 8, both), axis=0)
            power[rows, here] = part.astype(bf16)
        inverse = 1.0 / jnp.sum(total, axis=0, keepdims=True)
        found = jnp.dot(value_cols[...], power[:, here], preferred_element_type=f32) * inverse
        found = found.astype(bf16)
        grad_cols = grad_rows.T
        delta = jnp.sum(grad_cols.astype(f32) * found.astype(f32), axis=0, keepdims=True)
        for slot in range(span):
            rows = pl.ds(slot * tokens, tokens)
            d_probs = transposed_product(value_rows[rows, :], grad_rows)
            d_score[rows, here] = power[rows, here] * (d_probs - delta).astype(bf16)
        q_part = jnp.dot(key_cols[...], d_score[:, here], preferred_element_type=f32)
        q_part = (q_part * (inverse * scale)).T
        found = found.T
        column = jnp.broadcast_to(inverse, (head_dim, both)).T
        query_all[here, :] = (query_rows.astype(f32) * (column * scale)).astype(bf16)
        grad_all[here, :] = (grad_rows.astype(f32) * column).astype(bf16)
        for n in range(HEAD_GROUP):
            c = pl.ds((group * HEAD_GROUP + n) * head_dim, head_dim)
            rows = slice(n * tokens, (n + 1) * tokens)
            attended[:, c] = found[rows]
            q_grad[:, c] = q_part[rows]
            head = group * HEAD_GROUP + n
            sums[head // 2 : head // 2 + 1, head % 2 * head_dim : (head % 2 + 1) * head_dim] = (
                jnp.sum(q_part[rows], axis=0, keepdims=True)
            )

    groups = width // (HEAD_GROUP * head_dim)
    ready = scored(0)
    for group in range(groups):
        following = scored(group + 1) if group + 1 < groups else None
        finished(group, *ready)
        ready = following

    value_sum = jnp.zeros((1, head_dim), f32)
    for slot in range(span):
        rows = pl.ds(slot * tokens, tokens)
        key_part = jnp.dot(d_score[rows, :], query_all[...], preferred_element_type=f32)
        value_part = jnp.dot(power[rows, :], grad_all[...], preferred_element_type=f32)
        partials[slot, :tokens, :head_dim] = key_part.astype(bf16)
        partials[slot, :tokens, head_dim:] = value_part.astype(bf16)
        value_sum += jnp.sum(value_part, axis=0, keepdims=True)
    full = width // pair
    sums[full : full + 1, :head_dim] = value_sum
    sums[full : full + 1, head_dim:] = jnp.zeros_like(value_sum)
    sums[full + 1 :, :] = jnp.zeros((SUM_ROWS // 2 - full - 1, pair), f32)
    high = sums[...].astype(bf16)
    low = (sums[...] - high.astype(f32)).astype(bf16)
    both_rows = jnp.concatenate([high, low], axis=0)
    for slot in range(span):
        partials[slot, tokens:, :] = both_rows


def attention(place, queries, out_grad, window, bias):
    tokens, width = queries.shape
    span, _, pair = window.shape
    head_dim = pair // 2
    reach = span * tokens
    vmem = pl.BlockSpec(memory_space=pltpu.VMEM)
    smem = pl.BlockSpec(memory_space=pltpu.SMEM)
    return pl.pallas_call(
        attention_kernel,
        out_shape=(
            jax.ShapeDtypeStruct((tokens, width), bf16),
            jax.ShapeDtypeStruct((tokens, width), f32),
            jax.ShapeDtypeStruct((span, tokens + SUM_ROWS, pair), bf16),
        ),
        in_specs=[smem] + [vmem] * 4,
        out_specs=(vmem,) * 3,
        scratch_shapes=[
            pltpu.VMEM((reach, head_dim), bf16),
            pltpu.VMEM((head_dim, reach), bf16),
            pltpu.VMEM((head_dim, reach), bf16),
            pltpu.VMEM((reach, tokens), f32),
            pltpu.VMEM((2, reach, HEAD_GROUP * tokens), f32),
            pltpu.VMEM((reach, width), bf16),
            pltpu.VMEM((reach, width), bf16),
            pltpu.VMEM((width, head_dim), bf16),
            pltpu.VMEM((width, head_dim), bf16),
            pltpu.VMEM((SUM_ROWS // 2, pair), f32),
        ],
        compiler_params=pltpu.CompilerParams(vmem_limit_bytes=40 * 1024 * 1024),
        cost_estimate=pl.CostEstimate(
            flops=12 * width * reach * tokens,
            bytes_accessed=4 * tokens * width * 2,
            transcendentals=reach * width,
        ),
        name="attention",
    )(place, queries, out_grad, window, bias)


def rotated(size, first):
    return [[(first + i) % size for i in range(size)]]


def exchanged(blocks, axis, first=0):
    return lax.all_to_all(
        blocks, axis, 0, 0, axis_index_groups=rotated(lax.axis_size(axis), first)
    )


def per_device(queries, keys, values, out_grad, q_bias, v_bias, doc_lengths):
    tokens, head_dim = keys.shape[1], keys.shape[2]
    width = queries.shape[2]
    groups = lax.axis_size("z") * lax.axis_size("y") // SPAN
    shard = lax.axis_index(SEQ)
    member = shard % SPAN
    place = jnp.concatenate([jnp.stack([shard, member]).astype(jnp.int32), doc_lengths[0]])
    bias = jnp.concatenate([q_bias, v_bias])[None]

    own = jnp.concatenate([keys[0], values[0]], axis=1)
    before = lax.ppermute(own, SEQ, [(i, i + SPAN) for i in range((groups - 1) * SPAN)])
    later = ((jnp.arange(SPAN) + MEMBER_FIRST) % SPAN >= member)[:, None, None]
    before, place, bias = lax.optimization_barrier((before, place, bias))
    window = among_members(jnp.where(later, own[None], before[None]), groups)

    attended, q_grad, partials = attention(place, queries[0], out_grad[0], window, bias)

    received = among_members(partials, groups)
    inverse = 1.0 / math.sqrt(groups * SPAN * tokens * lax.axis_size("rep"))
    sums = jnp.sum(received[:, tokens:].astype(f32), axis=0) * inverse
    sums = sums[: SUM_ROWS // 2] + sums[SUM_ROWS // 2 :]
    full = width // (2 * head_dim)
    sums = jnp.concatenate([sums[:full], sums[full : 2 * full, :head_dim]], axis=1)
    copies = jnp.broadcast_to(sums[None], (lax.axis_size("rep"),) + sums.shape)
    received = received[:, :tokens].astype(f32)
    mine = jnp.sum(jnp.where(later, received, 0.0), axis=0)
    others = jnp.sum(jnp.where(later, 0.0, received), axis=0).astype(bf16)
    copies, mine, others = lax.optimization_barrier((copies, mine, others))
    rep_sums = jnp.sum(exchanged(copies, "rep", REP_FIRST), axis=0)
    rep_sums, others = lax.optimization_barrier((rep_sums, others))
    returned = lax.ppermute(others, SEQ, [(i + SPAN, i) for i in range((groups - 1) * SPAN)])
    k_grad = mine[None, :, :head_dim] + returned[None, :, :head_dim].astype(f32)
    v_grad = mine[None, :, head_dim:] + returned[None, :, head_dim:].astype(f32)
    copies = jnp.broadcast_to(rep_sums[None], (groups,) + rep_sums.shape)
    rows = along_groups(copies, groups)
    q_total = jnp.sum(rows[:, :, : 2 * head_dim], axis=0).reshape(width)
    v_total = jnp.sum(rows[:, 0, 2 * head_dim :], axis=0)
    return (
        attended[None],
        q_grad[None],
        k_grad,
        v_grad,
        q_total,
        v_total,
    )


def among_members(blocks, groups):
    order = rotated(SPAN, MEMBER_FIRST)[0]
    return lax.all_to_all(
        blocks, SEQ, 0, 0, axis_index_groups=[[g * SPAN + m for m in order] for g in range(groups)]
    )


def along_groups(blocks, groups):
    order = rotated(groups, groups * LINE_FIRST // 8)[0]
    return lax.all_to_all(
        blocks, SEQ, 0, 0, axis_index_groups=[[g * SPAN + m for g in order] for m in range(SPAN)]
    )


def solution(mesh):
    seq, rep = mesh.shape["seq"], mesh.shape["rep"]
    fine = Mesh(mesh.devices.reshape(2 * seq // SPAN, SPAN // 2, rep), ("z", "y", "rep"))
    tokens = P("rep", SEQ, None)
    return jax.shard_map(
        per_device,
        mesh=fine,
        in_specs=(tokens, tokens, tokens, tokens, P(), P(), P("rep", None)),
        out_specs=(tokens, tokens, tokens, tokens, P(), P()),
        check_vma=False,
    )
```
